256 devices in a mesh: dom: 8 (over z), row: 16 (over y, x), col: 2 (over core).
Axes of the slice: x: 4, y: 4, z: 8, core: 2. Of those that a mesh axis runs over, the one named last changes fastest.
Arguments:
- next_inverse: bfloat16 [8, 4096, 4096], P('dom', 'row', 'col'), may hold values from -6 to 6
- next_arrow: bfloat16 [8, 64, 4096], P('dom', None, 'row'), may hold values from -6 to 6
- factor_win: bfloat16 [8, 4096, 3072], P('dom', 'row', 'col'), may hold values from -0.09375 to 0.09375
- factor_rest: bfloat16 [8, 4096, 1024], P('dom', 'row', 'col'), may hold values from -0.09375 to 0.09375
- arrow_win: bfloat16 [8, 64, 3072], P('dom', None, 'col'), may hold values from -0.75 to 0.75
- arrow_rest: bfloat16 [8, 64, 1024], P('dom', None, 'col'), may hold values from -0.75 to 0.75
- tip_inverse: bfloat16 [64, 64], replicated, may hold values from -6 to 6
- base_win: bfloat16 [8, 3072, 3072], P('dom', 'row', 'col'), may hold values from -6 to 6
- base_rest: bfloat16 [8, 3072, 1024], P('dom', 'row', 'col'), may hold values from -6 to 6
Outputs:
- sub_inverse: bfloat16 [8, 4096, 3072], P('dom', 'row', 'col')
- arrow_inverse: bfloat16 [8, 64, 3072], P('dom', None, 'col')
- diag_win: bfloat16 [8, 3072, 3072], P('dom', 'row', 'col')
- diag_rest: bfloat16 [8, 3072, 1024], P('dom', 'row', 'col')
The draws below stay inside these ranges and needn't reach their ends.
All inputs are finite; a program needn't handle non-finite values.
Results may differ from the reference program's by a relative error of at most 0.0046.
Values may be sent and summed in bfloat16 or wider, within the bound.
A program may use at most 128 MiB of HBM per device.

```python
import jax
import jax.numpy as jnp
from jax import lax

NODES = 4096
ARROW = 64
WINDOW = 3072
PARTS_SIZE = 8


def level_of(stream_key, extent, cuts, smallest, high):
    factor_of, own = 1.0, jax.random.fold_in(stream_key, 6)
    for position, shards_of in cuts:
        steps = jnp.exp(jax.random.uniform(jax.random.fold_in(own, position), (shards_of,), jnp.float32, smallest / len(cuts), high / len(cuts)))
        factor_of = factor_of * jnp.repeat(steps, extent[position] // shards_of).reshape([-1 if axis == position else 1 for axis in range(len(extent))])
    return factor_of


def centred(own_key, shape, scale, reach, pieces=(), dtype=jnp.bfloat16):
    values = scale * jax.random.normal(own_key, shape, jnp.float32)
    if pieces:
        values = values * level_of(own_key, shape, pieces, -0.22, 0.18)
    return jnp.clip(values, -reach, reach).astype(dtype)


def setup_inputs(seed: int = 0) -> dict:
    splits = jax.random.split(jax.random.key(seed), 10)
    return {
        "next_inverse": centred(splits[0], (PARTS_SIZE, NODES, NODES), 1.0, 6.0, ((0, 8), (1, 16), (2, 2))),
        "next_arrow": centred(splits[1], (PARTS_SIZE, ARROW, NODES), 1.0, 6.0, ((0, 8), (2, 16))),
        "factor_win": centred(splits[2], (PARTS_SIZE, NODES, WINDOW), NODES ** -0.5, 0.09375, ((0, 8), (1, 16), (2, 2))),
        "factor_rest": centred(splits[3], (PARTS_SIZE, NODES, NODES - WINDOW), NODES ** -0.5, 0.09375, ((0, 8), (1, 16), (2, 2))),
        "arrow_win": centred(splits[4], (PARTS_SIZE, ARROW, WINDOW), ARROW ** -0.5, 0.75, ((0, 8), (2, 2))),
        "arrow_rest": centred(splits[5], (PARTS_SIZE, ARROW, NODES - WINDOW), ARROW ** -0.5, 0.75, ((0, 8), (2, 2))),
        "tip_inverse": centred(splits[6], (ARROW, ARROW), 1.0, 6.0),
        "base_win": centred(splits[7], (PARTS_SIZE, WINDOW, WINDOW), 1.0, 6.0, ((0, 8), (1, 16), (2, 2))),
        "base_rest": centred(splits[8], (PARTS_SIZE, WINDOW, NODES - WINDOW), 1.0, 6.0, ((0, 8), (1, 16), (2, 2))),
    }


def widen(value):
    return value.astype(jnp.float32)


def product(left, right):
    return jnp.dot(widen(left), widen(right), precision=lax.Precision.HIGHEST)


def one_partition(items):
    succ_inverse, succ_arrow, factor_a, factor_b, ratio_a, ratio_b, tip_inverse, base_a, base_b = items
    x_full = product(succ_inverse, factor_a) + product(succ_arrow.T, ratio_a)
    x_bf = x_full.astype(jnp.bfloat16)
    y_full = product(succ_arrow, factor_a) + product(tip_inverse, ratio_a)
    y_bf = y_full.astype(jnp.bfloat16)
    factor_all = jnp.concatenate([factor_a, factor_b], axis=1)
    ratio_all = jnp.concatenate([ratio_a, ratio_b], axis=1)
    base_all = widen(jnp.concatenate([base_a, base_b], axis=1))
    diag_full = base_all + product(x_bf.T, factor_all) + product(y_bf.T, ratio_all)
    split = factor_a.shape[1]
    return (-x_bf, -y_bf, diag_full[:, :split].astype(jnp.bfloat16), diag_full[:, split:].astype(jnp.bfloat16))


def reference(next_inverse, next_arrow, factor_win, factor_rest, arrow_win, arrow_rest, tip_inverse, base_win, base_rest):
    zero_inverse = jnp.zeros((1, NODES, NODES), jnp.bfloat16)
    zero_arrow = jnp.zeros((1, ARROW, NODES), jnp.bfloat16)
    succ_inverse = jnp.concatenate([next_inverse[1:], zero_inverse], axis=0)
    succ_arrow = jnp.concatenate([next_arrow[1:], zero_arrow], axis=0)
    tips = jnp.broadcast_to(tip_inverse, (PARTS_SIZE, ARROW, ARROW))
    return lax.map(one_partition, (succ_inverse, succ_arrow, factor_win, factor_rest, arrow_win, arrow_rest, tips, base_win, base_rest))
```

```python
import jax
import jax.numpy as jnp
from jax import lax
from jax.experimental import pallas as pl
from jax.experimental.pallas import tpu as pltpu
from jax.sharding import PartitionSpec as P

MESH = pl.DeviceIdType.MESH
BF16 = jnp.bfloat16
F32 = jnp.float32

BLOCK = 256
WIN = 1536
REST = 512
FULL = WIN + REST
ARROW = 64
DROWS = 192
TOP = 144
PIECE = 272
S_CHUNKS = 4
S_ROWS = BLOCK // S_CHUNKS
TILE = 256


def dot(left, right):
    return jnp.dot(left, right, preferred_element_type=F32)


def al(value, multiple):
    return pl.multiple_of(value, multiple)


def kernel(
    s_in, r_in, fw_in, fr_in, aw_in, ar_in, tip_in, bw_in, br_in,
    x_out, y_out, dw_out, dr_out,
    sz, rz, sg, fg, av, tip, base,
    x_send, x_hold, x_relay, x_recv, x_own, x_neg, xt, xg,
    y_all, yt, y_neg,
    d_send, d_hold, d_relay, d_recv, d_own, dw, dr,
    loc_sem, z_send, z_recv, f_send, f_recv, r_send, r_recv, sa_send, sa_recv,
    xr_send, xr_recv, xa_send, xa_recv, y_send, y_recv, t_send, t_recv,
    dr_send, dr_recv, out_sem,
):
    z = lax.axis_index("dom")
    row = lax.axis_index("row")
    k = lax.axis_index("col")
    y = row // 4
    x = row % 4
    a = (1 - k) * y + k * x
    b = (1 - k) * x + k * y
    stride_a = 4 - 3 * k
    stride_b = 1 + 3 * k

    def at(a_pos, b_pos):
        return {"row": a_pos * stride_a + b_pos * stride_b, "col": k}

    a_next, a_prev = (a + 1) % 4, (a + 3) % 4
    b_next, b_prev, b_opp = (b + 1) % 4, (b + 3) % 4, (b + 2) % 4

    pending = []

    def remote(src, dst, send_sem, recv_sem, device):
        copy = pltpu.make_async_remote_copy(
            src_ref=src, dst_ref=dst, send_sem=send_sem, recv_sem=recv_sem,
            device_id=device, device_id_type=MESH,
        )
        copy.start()
        pending.append((copy, None))
        return copy

    def remote_or_local(src, dst, send_sem, recv_sem, device, here, keep=True):
        copy = pltpu.make_async_remote_copy(
            src_ref=src, dst_ref=dst, send_sem=send_sem, recv_sem=recv_sem,
            device_id=device, device_id_type=MESH,
        )

        @pl.when(here)
        def _():
            pltpu.make_async_copy(src, dst, recv_sem).start()

        @pl.when(jnp.logical_not(here))
        def _():
            copy.start()

        if keep:
            pending.append((copy, here))

    def arrived(ref, sem):
        pltpu.make_async_copy(ref, ref, sem).wait()

    barrier = pltpu.get_barrier_semaphore()
    greeted = 0
    for step in (1, 7):
        pl.semaphore_signal(barrier, inc=1, device_id={"dom": (z + step) % 8}, device_id_type=MESH)
        greeted += 1
    pl.semaphore_signal(barrier, inc=1, device_id={"col": 1 - k}, device_id_type=MESH)
    greeted += 1
    for step in (1, 2, 3):
        for core in (0, 1):
            pl.semaphore_signal(
                barrier, inc=1, device_id={"row": y * 4 + (x + step) % 4, "col": core}, device_id_type=MESH
            )
            pl.semaphore_signal(
                barrier, inc=1, device_id={"row": ((y + step) % 4) * 4 + x, "col": core}, device_id_type=MESH
            )
            greeted += 2

    own_rows = pl.ds(al(a * BLOCK, BLOCK), BLOCK)
    locals_ = [
        pltpu.make_async_copy(fw_in, fg.at[own_rows, pl.ds(0, WIN)], loc_sem.at[0]),
        pltpu.make_async_copy(fr_in, fg.at[own_rows, pl.ds(WIN, REST)], loc_sem.at[1]),
        pltpu.make_async_copy(aw_in, av.at[:, pl.ds(0, WIN)], loc_sem.at[2]),
        pltpu.make_async_copy(ar_in, av.at[:, pl.ds(WIN, REST)], loc_sem.at[3]),
        pltpu.make_async_copy(tip_in, tip, loc_sem.at[4]),
        pltpu.make_async_copy(bw_in, base.at[:, pl.ds(0, WIN)], loc_sem.at[5]),
        pltpu.make_async_copy(br_in, base.at[:, pl.ds(WIN, REST)], loc_sem.at[6]),
    ]
    for copy in locals_:
        copy.start()

    pl.semaphore_wait(barrier, greeted)

    below = {"dom": (z + 7) % 8}
    z_copies = [remote(r_in, rz, z_send.at[S_CHUNKS], z_recv.at[S_CHUNKS], below)]
    for chunk in range(S_CHUNKS):
        rows = pl.ds(chunk * S_ROWS, S_ROWS)
        z_copies.append(remote(s_in.at[rows, :], sz.at[rows, :], z_send.at[chunk], z_recv.at[chunk], below))

    half = BLOCK // 2

    def block_half(a_pos, part, first, count):
        return fg.at[pl.ds(al(a_pos * BLOCK + part * half, half), half), pl.ds(first, count)]

    def f_own(source, first, count, base_sem):
        for part in (0, 1):
            src = source.at[pl.ds(part * half, half), :]
            remote(src, block_half(a, part, first, count), f_send.at[base_sem + part],
                   f_recv.at[base_sem + part], at(a_next, b))
            src = source.at[pl.ds((1 - part) * half, half), :]
            remote(src, block_half(a, 1 - part, first, count), f_send.at[base_sem + 3 - part],
                   f_recv.at[base_sem + 3 - part], at(a_prev, b))

    def f_forward(first, count, base_sem):
        block = block_half(a_prev, 0, first, count)
        arrived(block, f_recv.at[base_sem])
        remote(block, block, f_send.at[base_sem + 4], f_recv.at[base_sem + 4], at(a_next, b))
        block = block_half(a_next, 1, first, count)
        arrived(block, f_recv.at[base_sem + 3])
        remote(block, block, f_send.at[base_sem + 5], f_recv.at[base_sem + 5], at(a_prev, b))

    def f_rest_of(first, count, base_sem):
        arrived(block_half(a_prev, 1, first, count), f_recv.at[base_sem + 1])
        arrived(block_half(a_next, 0, first, count), f_recv.at[base_sem + 2])
        far = (a + 2) % 4
        arrived(block_half(far, 0, first, count), f_recv.at[base_sem + 4])
        arrived(block_half(far, 1, first, count), f_recv.at[base_sem + 5])

    f_own(fw_in, 0, WIN, 0)

    arrived(rz, z_recv.at[S_CHUNKS])

    @pl.when(z == 7)
    def _():
        rz[...] = jnp.zeros_like(rz)

    r_dst = sg.at[:, pl.ds(128, 16), pl.ds(al(a * BLOCK, BLOCK), BLOCK)]
    for step in (1, 2, 3):
        remote(rz, r_dst, r_send.at[step - 1], r_recv, at((a + step) % 4, b))
    pltpu.make_async_copy(rz, r_dst, r_recv).start()

    def s_spread(chunk):
        first = chunk * S_ROWS
        rows = pl.ds(first, S_ROWS)
        into = pl.ds(first + 16 * (first // 128), S_ROWS)
        arrived(sz.at[rows, :], z_recv.at[chunk])

        @pl.when(z == 7)
        def _():
            sz[rows, :] = jnp.zeros((S_ROWS, 2048), BF16)

        index = 0
        for step in range(4):
            x_to = (x + step) % 4
            for part in range(2):
                src = sz.at[rows, pl.ds(al((part * 4 + x_to) * BLOCK, BLOCK), BLOCK)]
                dst = sg.at[x, into, pl.ds(al((2 * k + part) * BLOCK, BLOCK), BLOCK)]
                device = {"row": y * 4 + x_to, "col": 0}
                sems = (sa_send.at[chunk, index], sa_recv.at[x], device)
                if step:
                    remote(src, dst, *sems)
                else:
                    remote_or_local(src, dst, *sems, k == 0)
                index += 1
        for part in range(2):
            y_to = 2 * k + part
            src = sz.at[rows, pl.ds(part * 1024, 1024)]
            dst = sg.at[y, into, :]
            device = {"row": y_to * 4 + x, "col": 1}
            here = jnp.logical_and(y_to == y, k == 1)
            remote_or_local(src, dst, sa_send.at[chunk, index], sa_recv.at[y], device, here)
            index += 1

    s_spread(0)
    f_forward(0, WIN, 0)
    s_spread(1)
    s_spread(2)
    f_own(fr_in, WIN, REST, 6)
    s_spread(3)
    f_forward(WIN, REST, 6)

    for copy in locals_:
        copy.wait()
    f_rest_of(0, WIN, 0)
    arrived(sg.at[:, pl.ds(128, 16), :], r_recv)

    def reduce_scatter(chunks, width, top, piece, product, send, hold, relay, recv, s_sem, r_sem, ready):
        def part_of(ref, lead, upper, cols):
            rows = pl.ds(0, top) if upper else pl.ds(top, piece - top)
            return ref.at[lead, rows, cols] if lead is not None else ref.at[rows, cols]

        def opposite(c):
            def body(n, _):
                cols = pl.ds(al(c * width + n * TILE, TILE), TILE)
                send[0, :, cols] = product(b_opp, cols).astype(BF16)
                return 0

            lax.fori_loop(0, width // TILE, body, 0)
            cols = pl.ds(c * width, width)
            remote(part_of(send, 0, True, cols), part_of(relay, None, True, cols),
                   s_sem.at[c, 0], r_sem.at[c, 0], at(a, b_next))
            remote(part_of(send, 0, False, cols), part_of(relay, None, False, cols),
                   s_sem.at[c, 1], r_sem.at[c, 1], at(a, b_prev))

        def beside(c):
            def body_next(n, _):
                cols = pl.ds(al(c * width + n * TILE, TILE), TILE)
                value = product(b_next, cols)
                hold[pl.ds(0, top), cols] = value[:top]
                send[1, pl.ds(top, piece - top), cols] = value[top:].astype(BF16)
                return 0

            def body_prev(n, _):
                cols = pl.ds(al(c * width + n * TILE, TILE), TILE)
                value = product(b_prev, cols)
                hold[pl.ds(top, piece - top), cols] = value[top:]
                send[2, pl.ds(0, top), cols] = value[:top].astype(BF16)
                return 0

            cols = pl.ds(c * width, width)
            lax.fori_loop(0, width // TILE, body_next, 0)
            remote(part_of(send, 1, False, cols), part_of(recv, 0, False, cols),
                   s_sem.at[c, 2], r_sem.at[c, 2], at(a, b_next))
            lax.fori_loop(0, width // TILE, body_prev, 0)
            remote(part_of(send, 2, True, cols), part_of(recv, 1, True, cols),
                   s_sem.at[c, 3], r_sem.at[c, 3], at(a, b_prev))

        def relayed(c):
            cols = pl.ds(c * width, width)
            arrived(part_of(relay, None, True, cols), r_sem.at[c, 0])
            rows = pl.ds(0, top)
            send[1, rows, cols] = (hold[rows, cols] + relay[rows, cols].astype(F32)).astype(BF16)
            remote(part_of(send, 1, True, cols), part_of(recv, 0, True, cols),
                   s_sem.at[c, 4], r_sem.at[c, 4], at(a, b_next))
            arrived(part_of(relay, None, False, cols), r_sem.at[c, 1])
            rows = pl.ds(top, piece - top)
            send[2, rows, cols] = (hold[rows, cols] + relay[rows, cols].astype(F32)).astype(BF16)
            remote(part_of(send, 2, False, cols), part_of(recv, 1, False, cols),
                   s_sem.at[c, 5], r_sem.at[c, 5], at(a, b_prev))

        def received(c):
            cols = pl.ds(c * width, width)
            arrived(part_of(recv, 0, False, cols), r_sem.at[c, 2])
            arrived(part_of(recv, 1, True, cols), r_sem.at[c, 3])
            arrived(part_of(recv, 0, True, cols), r_sem.at[c, 4])
            arrived(part_of(recv, 1, False, cols), r_sem.at[c, 5])

        return opposite, beside, relayed, received

    def x_product(b_pos, cols):
        return dot(sg[b_pos], fg[:, cols])

    x_width = 768
    opposite, beside, relayed, received = reduce_scatter(
        2, x_width, TOP, PIECE, x_product, x_send, x_hold, x_relay, x_recv, xr_send, xr_recv, None
    )

    def x_here(c):
        def body(n, _):
            cols = pl.ds(al(c * x_width + n * TILE, TILE), TILE)
            value = x_product(b, cols)
            arrow = lax.dot_general(
                rz[...].reshape(ARROW, BLOCK), av[:, cols], (((0,), (0,)), ((), ())),
                preferred_element_type=F32,
            )
            mine = tip[pl.ds(al(b * 16, 16), 16), :]
            x_own[pl.ds(0, 128), cols] = value[:128] + arrow[:128]
            x_own[pl.ds(128, 16), cols] = value[128:TOP] + dot(mine, av[:, cols])
            x_own[pl.ds(TOP, 128), cols] = value[TOP:] + arrow[128:]
            return 0

        lax.fori_loop(0, x_width // TILE, body, 0)

    y_rows = pl.ds(al(b * 16, 16), 16)

    def x_final(c):
        received(c)

        def body(n, _):
            cols = pl.ds(al(c * x_width + n * TILE, TILE), TILE)
            total = x_own[:, cols] + x_recv[0, :, cols].astype(F32) + x_recv[1, :, cols].astype(F32)
            top = total[:128].astype(BF16)
            bottom = total[TOP:].astype(BF16)
            x_neg[pl.ds(0, 128), cols] = -top
            x_neg[pl.ds(128, 128), cols] = -bottom
            xt[cols, pl.ds(0, 128)] = top.T
            xt[cols, pl.ds(128, 128)] = bottom.T
            y_all[k, y_rows, cols] = total[128:TOP].astype(BF16)
            return 0

        lax.fori_loop(0, x_width // TILE, body, 0)
        y_to = 2 * k + c
        here = jnp.logical_and(y_to == y, k == 0)
        remote_or_local(
            xt.at[pl.ds(c * 768, 768), :], xg.at[:, pl.ds(al(y * BLOCK, BLOCK), BLOCK)],
            xa_send.at[c, 0], xa_recv.at[y], {"row": y_to * 4 + x, "col": 0}, here,
        )
        for step in range(4):
            x_to = (x + step) % 4
            src = xt.at[pl.ds(al(c * 768 + x_to * DROWS, 64), DROWS), :]
            dst = xg.at[pl.ds(al(y_to * DROWS, 64), DROWS), pl.ds(al(x * BLOCK, BLOCK), BLOCK)]
            sems = (xa_send.at[c, 1 + step], xa_recv.at[x], {"row": y * 4 + x_to, "col": 1})
            if step:
                remote(src, dst, *sems)
            else:
                remote_or_local(src, dst, *sems, k == 1)

    arrived(sg.at[b_opp, pl.ds(0, BLOCK), :], sa_recv.at[b_opp])
    opposite(0)
    arrived(sg.at[b_next, pl.ds(0, BLOCK), :], sa_recv.at[b_next])
    arrived(sg.at[b_prev, pl.ds(0, BLOCK), :], sa_recv.at[b_prev])
    beside(0)
    opposite(1)
    relayed(0)
    beside(1)
    arrived(sg.at[b, pl.ds(0, BLOCK), :], sa_recv.at[b])
    x_here(0)
    relayed(1)
    x_here(1)
    x_final(0)
    x_final(1)
    outs = [pltpu.make_async_copy(x_neg, x_out, out_sem.at[0])]
    outs[0].start()

    y_mine = y_all.at[k, y_rows, :]
    for step in (1, 2, 3):
        remote(y_mine, y_mine, y_send.at[step - 1], y_recv.at[step - 1], at(a, (b + step) % 4))

    f_rest_of(WIN, REST, 6)
    for a_pos in range(4):
        arrived(xg.at[:, pl.ds(a_pos * BLOCK, BLOCK)], xa_recv.at[a_pos])

    def d_product(b_pos, cols):
        return dot(xg[pl.ds(al(b_pos * DROWS, 64), DROWS), :], fg[:, cols])

    d_width = 1024
    opposite, beside, relayed, received = reduce_scatter(
        2, d_width, DROWS // 2, DROWS, d_product, d_send, d_hold, d_relay, d_recv, dr_send, dr_recv, None
    )
    opposite(0)
    beside(0)
    opposite(1)
    for step in (1, 2, 3):
        theirs = y_all.at[k, pl.ds(al(((b + 4 - step) % 4) * 16, 16), 16), :]
        arrived(theirs, y_recv.at[step - 1])
    remote(y_all.at[k], y_all.at[k], t_send, t_recv, {"col": 1 - k})
    relayed(0)
    beside(1)
    y_neg[...] = -y_all[k]
    outs.append(pltpu.make_async_copy(y_neg, y_out, out_sem.at[1]))
    outs[1].start()
    arrived(y_all.at[1 - k], t_recv)
    yt[...] = y_all[row // 8].T

    def d_here(c):
        def body(n, _):
            cols = pl.ds(al(c * d_width + n * TILE, TILE), TILE)
            value = d_product(b, cols)
            mine = yt[pl.ds(al((row % 8) * DROWS, 64), DROWS), :]
            d_own[:, cols] = value + base[:, cols].astype(F32) + dot(mine, av[:, cols])
            return 0

        lax.fori_loop(0, d_width // TILE, body, 0)

    d_here(0)
    relayed(1)
    d_here(1)

    received(0)
    cols = pl.ds(0, d_width)
    dw[:, cols] = (d_own[:, cols] + d_recv[0, :, cols].astype(F32) + d_recv[1, :, cols].astype(F32)).astype(BF16)
    received(1)
    cols = pl.ds(d_width, WIN - d_width)
    dw[:, cols] = (d_own[:, cols] + d_recv[0, :, cols].astype(F32) + d_recv[1, :, cols].astype(F32)).astype(BF16)
    outs.append(pltpu.make_async_copy(dw, dw_out, out_sem.at[2]))
    outs[2].start()
    cols = pl.ds(WIN, REST)
    dr[...] = (d_own[:, cols] + d_recv[0, :, cols].astype(F32) + d_recv[1, :, cols].astype(F32)).astype(BF16)
    outs.append(pltpu.make_async_copy(dr, dr_out, out_sem.at[3]))
    outs[3].start()

    for copy, here in pending:
        if here is None:
            copy.wait_send()
        else:
            pl.when(jnp.logical_not(here))(copy.wait_send)
    for copy in outs:
        copy.wait()


def per_device(s, r, fw, fr, aw, ar, tip, bw, br):
    hbm = pl.BlockSpec(memory_space=pl.ANY)
    vmem = pltpu.VMEM
    dma = pltpu.SemaphoreType.DMA
    outs = pl.pallas_call(
        kernel,
        out_shape=(
            jax.ShapeDtypeStruct((BLOCK, WIN), BF16),
            jax.ShapeDtypeStruct((ARROW, WIN), BF16),
            jax.ShapeDtypeStruct((DROWS, WIN), BF16),
            jax.ShapeDtypeStruct((DROWS, REST), BF16),
        ),
        in_specs=[hbm] * 9,
        out_specs=(hbm,) * 4,
        scratch_shapes=[
            vmem((BLOCK, 2048), BF16),
            vmem((4, 16, BLOCK), BF16),
            vmem((4, PIECE, 1024), BF16),
            vmem((1024, FULL), BF16),
            vmem((ARROW, FULL), BF16),
            vmem((ARROW, ARROW), BF16),
            vmem((DROWS, FULL), BF16),
            vmem((3, PIECE, WIN), BF16),
            vmem((PIECE, WIN), F32),
            vmem((PIECE, WIN), BF16),
            vmem((2, PIECE, WIN), BF16),
            vmem((PIECE, WIN), F32),
            vmem((BLOCK, WIN), BF16),
            vmem((WIN, BLOCK), BF16),
            vmem((768, 1024), BF16),
            vmem((2, ARROW, WIN), BF16),
            vmem((WIN, ARROW), BF16),
            vmem((ARROW, WIN), BF16),
            vmem((3, DROWS, FULL), BF16),
            vmem((DROWS, FULL), F32),
            vmem((DROWS, FULL), BF16),
            vmem((2, DROWS, FULL), BF16),
            vmem((DROWS, FULL), F32),
            vmem((DROWS, WIN), BF16),
            vmem((DROWS, REST), BF16),
            dma((7,)),
            dma((S_CHUNKS + 1,)), dma((S_CHUNKS + 1,)),
            dma((12,)), dma((12,)),
            dma((3,)), dma,
            dma((S_CHUNKS, 10)), dma((4,)),
            dma((2, 6)), dma((2, 6)),
            dma((2, 5)), dma((4,)),
            dma((3,)), dma((3,)),
            dma, dma,
            dma((2, 6)), dma((2, 6)),
            dma((4,)),
        ],
        compiler_params=pltpu.CompilerParams(
            collective_id=0, has_side_effects=True, vmem_limit_bytes=60 << 20
        ),
        cost_estimate=pl.CostEstimate(flops=6_800_000_000, bytes_accessed=8_000_000, transcendentals=0),
    )(s[0], r[0].reshape(4, 16, BLOCK), fw[0], fr[0], aw[0], ar[0], tip, bw[0], br[0])
    return tuple(value[None] for value in outs)


def solution(mesh):
    in_specs = (
        P("dom", "row", "col"),
        P("dom", None, "row"),
        P("dom", "row", "col"),
        P("dom", "row", "col"),
        P("dom", None, "col"),
        P("dom", None, "col"),
        P(),
        P("dom", "row", "col"),
        P("dom", "row", "col"),
    )
    out_specs = (
        P("dom", "row", "col"),
        P("dom", None, "col"),
        P("dom", "row", "col"),
        P("dom", "row", "col"),
    )
    return jax.shard_map(
        per_device, mesh=mesh, in_specs=in_specs, out_specs=out_specs, check_vma=False
    )
```

```python
import jax
import jax.numpy as jnp
from jax import lax
from jax.experimental import pallas as pl
from jax.experimental.pallas import tpu as pltpu
from jax.sharding import PartitionSpec as P

MESH = pl.DeviceIdType.MESH
BF16 = jnp.bfloat16
F32 = jnp.float32

BLOCK = 256
WIN = 1536
REST = 512
FULL = WIN + REST
ARROW = 64
DROWS = 192
TOP = 144
PIECE = 272
S_CHUNKS = 4
S_ROWS = BLOCK // S_CHUNKS
TILE = 256


def dot(left, right):
    return jnp.dot(left, right, preferred_element_type=F32)


def al(value, multiple):
    return pl.multiple_of(value, multiple)


def kernel(
    s_in, r_in, fw_in, fr_in, aw_in, ar_in, tip_in, bw_in, br_in,
    x_out, y_out, dw_out, dr_out,
    sz, rz, sg, fg, av, tip, base,
    x_send, x_hold, x_relay, x_recv, x_own, x_neg, xt, xg,
    y_all, yt, y_neg,
    d_send, d_hold, d_relay, d_recv, d_own, dw, dr,
    loc_sem, z_send, z_recv, f_send, f_recv, r_send, r_recv, sa_send, sa_recv,
    xr_send, xr_recv, xa_send, xa_recv, y_send, y_recv, t_send, t_recv,
    dr_send, dr_recv, out_sem,
):
    z = lax.axis_index("dom")
    row = lax.axis_index("row")
    k = lax.axis_index("col")
    y = row // 4
    x = row % 4
    a = (1 - k) * y + k * x
    b = (1 - k) * x + k * y
    stride_a = 4 - 3 * k
    stride_b = 1 + 3 * k

    def at(a_pos, b_pos):
        return {"row": a_pos * stride_a + b_pos * stride_b, "col": k}

    a_next, a_prev = (a + 1) % 4, (a + 3) % 4
    b_next, b_prev, b_opp = (b + 1) % 4, (b + 3) % 4, (b + 2) % 4

    pending = []

    def remote(src, dst, send_sem, recv_sem, device):
        copy = pltpu.make_async_remote_copy(
            src_ref=src, dst_ref=dst, send_sem=send_sem, recv_sem=recv_sem,
            device_id=device, device_id_type=MESH,
        )
        copy.start()
        pending.append((copy, None))
        return copy

    def remote_or_local(src, dst, send_sem, recv_sem, device, here, keep=True):
        copy = pltpu.make_async_remote_copy(
            src_ref=src, dst_ref=dst, send_sem=send_sem, recv_sem=recv_sem,
            device_id=device, device_id_type=MESH,
        )

        @pl.when(here)
        def _():
            pltpu.make_async_copy(src, dst, recv_sem).start()

        @pl.when(jnp.logical_not(here))
        def _():
            copy.start()

        if keep:
            pending.append((copy, here))

    def arrived(ref, sem):
        pltpu.make_async_copy(ref, ref, sem).wait()

    barrier = pltpu.get_barrier_semaphore()
    greeted = 0
    for step in (1, 7):
        pl.semaphore_signal(barrier, inc=1, device_id={"dom": (z + step) % 8}, device_id_type=MESH)
        greeted += 1
    pl.semaphore_signal(barrier, inc=1, device_id={"col": 1 - k}, device_id_type=MESH)
    greeted += 1
    for step in (1, 2, 3):
        for core in (0, 1):
            pl.semaphore_signal(
                barrier, inc=1, device_id={"row": y * 4 + (x + step) % 4, "col": core}, device_id_type=MESH
            )
            pl.semaphore_signal(
                barrier, inc=1, device_id={"row": ((y + step) % 4) * 4 + x, "col": core}, device_id_type=MESH
            )
            greeted += 2

    own_rows = pl.ds(al(a * BLOCK, BLOCK), BLOCK)
    locals_ = [
        pltpu.make_async_copy(fw_in, fg.at[own_rows, pl.ds(0, WIN)], loc_sem.at[0]),
        pltpu.make_async_copy(fr_in, fg.at[own_rows, pl.ds(WIN, REST)], loc_sem.at[1]),
        pltpu.make_async_copy(aw_in, av.at[:, pl.ds(0, WIN)], loc_sem.at[2]),
        pltpu.make_async_copy(ar_in, av.at[:, pl.ds(WIN, REST)], loc_sem.at[3]),
        pltpu.make_async_copy(tip_in, tip, loc_sem.at[4]),
        pltpu.make_async_copy(bw_in, base.at[:, pl.ds(0, WIN)], loc_sem.at[5]),
        pltpu.make_async_copy(br_in, base.at[:, pl.ds(WIN, REST)], loc_sem.at[6]),
    ]
    for copy in locals_:
        copy.start()

    pl.semaphore_wait(barrier, greeted)

    below = {"dom": (z + 7) % 8}
    remote(r_in, rz, z_send.at[S_CHUNKS], z_recv.at[S_CHUNKS], below)
    z_copies = []

    def z_start(chunk):
        rows = pl.ds(chunk * S_ROWS, S_ROWS)
        z_copies.append(remote(s_in.at[rows, :], sz.at[rows, :], z_send.at[chunk], z_recv.at[chunk], below))

    z_start(0)
    z_start(1)

    half = BLOCK // 2

    def block_half(a_pos, part, first, count):
        return fg.at[pl.ds(al(a_pos * BLOCK + part * half, half), half), pl.ds(first, count)]

    def f_own(source, first, count, base_sem):
        for part in (0, 1):
            src = source.at[pl.ds(part * half, half), :]
            remote(src, block_half(a, part, first, count), f_send.at[base_sem + part],
                   f_recv.at[base_sem + part], at(a_next, b))
            src = source.at[pl.ds((1 - part) * half, half), :]
            remote(src, block_half(a, 1 - part, first, count), f_send.at[base_sem + 3 - part],
                   f_recv.at[base_sem + 3 - part], at(a_prev, b))

    def f_forward(first, count, base_sem):
        block = block_half(a_prev, 0, first, count)
        arrived(block, f_recv.at[base_sem])
        remote(block, block, f_send.at[base_sem + 4], f_recv.at[base_sem + 4], at(a_next, b))
        block = block_half(a_next, 1, first, count)
        arrived(block, f_recv.at[base_sem + 3])
        remote(block, block, f_send.at[base_sem + 5], f_recv.at[base_sem + 5], at(a_prev, b))

    def f_rest_of(first, count, base_sem):
        arrived(block_half(a_prev, 1, first, count), f_recv.at[base_sem + 1])
        arrived(block_half(a_next, 0, first, count), f_recv.at[base_sem + 2])
        far = (a + 2) % 4
        arrived(block_half(far, 0, first, count), f_recv.at[base_sem + 4])
        arrived(block_half(far, 1, first, count), f_recv.at[base_sem + 5])

    f_own(fw_in, 0, WIN, 0)

    arrived(rz, z_recv.at[S_CHUNKS])

    @pl.when(z == 7)
    def _():
        rz[...] = jnp.zeros_like(rz)

    r_dst = sg.at[:, pl.ds(128, 16), pl.ds(al(a * BLOCK, BLOCK), BLOCK)]
    for step in (1, 2, 3):
        remote(rz, r_dst, r_send.at[step - 1], r_recv, at((a + step) % 4, b))
    pltpu.make_async_copy(rz, r_dst, r_recv).start()

    def s_spread(chunk):
        first = chunk * S_ROWS
        rows = pl.ds(first, S_ROWS)
        into = pl.ds(first + 16 * (first // 128), S_ROWS)
        arrived(sz.at[rows, :], z_recv.at[chunk])
        if chunk + 2 < S_CHUNKS:
            z_copies[chunk].wait_send()
            pending[:] = [item for item in pending if item[0] is not z_copies[chunk]]
            z_start(chunk + 2)

        @pl.when(z == 7)
        def _():
            sz[rows, :] = jnp.zeros((S_ROWS, 2048), BF16)

        index = 0
        for step in range(4):
            x_to = (x + step) % 4
            for part in range(2):
                src = sz.at[rows, pl.ds(al((part * 4 + x_to) * BLOCK, BLOCK), BLOCK)]
                dst = sg.at[x, into, pl.ds(al((2 * k + part) * BLOCK, BLOCK), BLOCK)]
                device = {"row": y * 4 + x_to, "col": 0}
                sems = (sa_send.at[chunk, index], sa_recv.at[x], device)
                if step:
                    remote(src, dst, *sems)
                else:
                    remote_or_local(src, dst, *sems, k == 0)
                index += 1
        for part in range(2):
            y_to = 2 * k + part
            src = sz.at[rows, pl.ds(part * 1024, 1024)]
            dst = sg.at[y, into, :]
            device = {"row": y_to * 4 + x, "col": 1}
            here = jnp.logical_and(y_to == y, k == 1)
            remote_or_local(src, dst, sa_send.at[chunk, index], sa_recv.at[y], device, here)
            index += 1

    s_spread(0)
    f_forward(0, WIN, 0)
    s_spread(1)
    s_spread(2)
    s_spread(3)
    f_own(fr_in, WIN, REST, 6)

    for copy in locals_:
        copy.wait()
    f_rest_of(0, WIN, 0)
    arrived(sg.at[:, pl.ds(128, 16), :], r_recv)

    def reduce_scatter(width, turn, top, piece, product, send, hold, relay, recv, s_sem, r_sem):
        def first_of(c):
            return al((c + turn) % 2 * width, TILE)

        def part_of(ref, lead, upper, cols):
            rows = pl.ds(0, top) if upper else pl.ds(top, piece - top)
            return ref.at[lead, rows, cols] if lead is not None else ref.at[rows, cols]

        def opposite(c):
            cols = pl.ds(first_of(c), width)
            send[0, :, cols] = product(b_opp, cols).astype(BF16)
            remote(part_of(send, 0, True, cols), part_of(relay, None, True, cols),
                   s_sem.at[c, 0], r_sem.at[c, 0], at(a, b_next))
            remote(part_of(send, 0, False, cols), part_of(relay, None, False, cols),
                   s_sem.at[c, 1], r_sem.at[c, 1], at(a, b_prev))

        def beside(c):
            cols = pl.ds(first_of(c), width)
            value = product(b_next, cols)
            hold[pl.ds(0, top), cols] = value[:top]
            send[1, pl.ds(top, piece - top), cols] = value[top:].astype(BF16)
            remote(part_of(send, 1, False, cols), part_of(recv, 0, False, cols),
                   s_sem.at[c, 2], r_sem.at[c, 2], at(a, b_next))
            value = product(b_prev, cols)
            hold[pl.ds(top, piece - top), cols] = value[top:]
            send[2, pl.ds(0, top), cols] = value[:top].astype(BF16)
            remote(part_of(send, 2, True, cols), part_of(recv, 1, True, cols),
                   s_sem.at[c, 3], r_sem.at[c, 3], at(a, b_prev))

        def relayed(c):
            cols = pl.ds(first_of(c), width)
            arrived(part_of(relay, None, True, cols), r_sem.at[c, 0])
            rows = pl.ds(0, top)
            send[1, rows, cols] = (hold[rows, cols] + relay[rows, cols].astype(F32)).astype(BF16)
            remote(part_of(send, 1, True, cols), part_of(recv, 0, True, cols),
                   s_sem.at[c, 4], r_sem.at[c, 4], at(a, b_next))
            arrived(part_of(relay, None, False, cols), r_sem.at[c, 1])
            rows = pl.ds(top, piece - top)
            send[2, rows, cols] = (hold[rows, cols] + relay[rows, cols].astype(F32)).astype(BF16)
            remote(part_of(send, 2, False, cols), part_of(recv, 1, False, cols),
                   s_sem.at[c, 5], r_sem.at[c, 5], at(a, b_prev))

        def received(c):
            cols = pl.ds(first_of(c), width)
            arrived(part_of(recv, 0, False, cols), r_sem.at[c, 2])
            arrived(part_of(recv, 1, True, cols), r_sem.at[c, 3])
            arrived(part_of(recv, 0, True, cols), r_sem.at[c, 4])
            arrived(part_of(recv, 1, False, cols), r_sem.at[c, 5])

        return opposite, beside, relayed, received

    def x_product(b_pos, cols):
        return dot(sg[b_pos], fg[:, cols])

    x_width = 768
    opposite, beside, relayed, received = reduce_scatter(
        x_width, a, TOP, PIECE, x_product, x_send, x_hold, x_relay, x_recv, xr_send, xr_recv
    )

    def x_here(c):
        cols = pl.ds(al((c + a) % 2 * x_width, TILE), x_width)
        value = x_product(b, cols)
        arrow = lax.dot_general(
            rz[...].reshape(ARROW, BLOCK), av[:, cols], (((0,), (0,)), ((), ())),
            preferred_element_type=F32,
        )
        mine = tip[pl.ds(al(b * 16, 16), 16), :]
        x_own[pl.ds(0, 128), cols] = value[:128] + arrow[:128]
        x_own[pl.ds(128, 16), cols] = value[128:TOP] + dot(mine, av[:, cols])
        x_own[pl.ds(TOP, 128), cols] = value[TOP:] + arrow[128:]

    y_rows = pl.ds(al(b * 16, 16), 16)

    def x_final(c):
        received(c)
        turn = (c + a) % 2
        first = turn * x_width

        def body(n, _):
            cols = pl.ds(al(first + n * TILE, TILE), TILE)
            total = x_own[:, cols] + x_recv[0, :, cols].astype(F32) + x_recv[1, :, cols].astype(F32)
            top = total[:128].astype(BF16)
            bottom = total[TOP:].astype(BF16)
            x_neg[pl.ds(0, 128), cols] = -top
            x_neg[pl.ds(128, 128), cols] = -bottom
            xt[cols, pl.ds(0, 128)] = top.T
            xt[cols, pl.ds(128, 128)] = bottom.T
            y_all[k, y_rows, cols] = total[128:TOP].astype(BF16)
            return 0

        lax.fori_loop(0, x_width // TILE, body, 0)
        y_to = 2 * k + turn
        here = jnp.logical_and(y_to == y, k == 0)
        remote_or_local(
            xt.at[pl.ds(al(first, TILE), x_width), :], xg.at[:, pl.ds(al(y * BLOCK, BLOCK), BLOCK)],
            xa_send.at[c, 0], xa_recv.at[y], {"row": y_to * 4 + x, "col": 0}, here,
        )
        for step in range(4):
            x_to = (x + step) % 4
            src = xt.at[pl.ds(al(first + x_to * DROWS, 64), DROWS), :]
            dst = xg.at[pl.ds(al(y_to * DROWS, 64), DROWS), pl.ds(al(x * BLOCK, BLOCK), BLOCK)]
            sems = (xa_send.at[c, 1 + step], xa_recv.at[x], {"row": y * 4 + x_to, "col": 1})
            if step:
                remote(src, dst, *sems)
            else:
                remote_or_local(src, dst, *sems, k == 1)

    arrived(sg.at[b_opp, pl.ds(0, BLOCK), :], sa_recv.at[b_opp])
    opposite(0)
    arrived(sg.at[b_next, pl.ds(0, BLOCK), :], sa_recv.at[b_next])
    arrived(sg.at[b_prev, pl.ds(0, BLOCK), :], sa_recv.at[b_prev])
    beside(0)
    opposite(1)
    f_forward(WIN, REST, 6)
    relayed(0)
    beside(1)
    arrived(sg.at[b, pl.ds(0, BLOCK), :], sa_recv.at[b])
    x_here(0)
    relayed(1)
    x_here(1)
    x_final(0)
    x_final(1)
    outs = [pltpu.make_async_copy(x_neg, x_out, out_sem.at[0])]
    outs[0].start()

    y_mine = y_all.at[k, y_rows, :]
    for step in (1, 2, 3):
        remote(y_mine, y_mine, y_send.at[step - 1], y_recv.at[step - 1], at(a, (b + step) % 4))

    f_rest_of(WIN, REST, 6)
    for a_pos in range(4):
        arrived(xg.at[:, pl.ds(a_pos * BLOCK, BLOCK)], xa_recv.at[a_pos])

    def d_product(b_pos, cols):
        return dot(xg[pl.ds(al(b_pos * DROWS, 64), DROWS), :], fg[:, cols])

    d_width = 1024
    opposite, beside, relayed, received = reduce_scatter(
        d_width, 0, DROWS // 2, DROWS, d_product, d_send, d_hold, d_relay, d_recv, dr_send, dr_recv
    )
    opposite(0)
    beside(0)
    opposite(1)
    for step in (1, 2, 3):
        theirs = y_all.at[k, pl.ds(al(((b + 4 - step) % 4) * 16, 16), 16), :]
        arrived(theirs, y_recv.at[step - 1])
    remote(y_all.at[k], y_all.at[k], t_send, t_recv, {"col": 1 - k})
    relayed(0)
    beside(1)
    y_neg[...] = -y_all[k]
    outs.append(pltpu.make_async_copy(y_neg, y_out, out_sem.at[1]))
    outs[1].start()
    arrived(y_all.at[1 - k], t_recv)
    yt[...] = y_all[row // 8].T

    def d_here(c):
        cols = pl.ds(c * d_width, d_width)
        value = d_product(b, cols)
        mine = yt[pl.ds(al((row % 8) * DROWS, 64), DROWS), :]
        d_own[:, cols] = value + base[:, cols].astype(F32) + dot(mine, av[:, cols])

    d_here(0)
    relayed(1)
    d_here(1)

    received(0)
    cols = pl.ds(0, d_width)
    dw[:, cols] = (d_own[:, cols] + d_recv[0, :, cols].astype(F32) + d_recv[1, :, cols].astype(F32)).astype(BF16)
    received(1)
    cols = pl.ds(d_width, WIN - d_width)
    dw[:, cols] = (d_own[:, cols] + d_recv[0, :, cols].astype(F32) + d_recv[1, :, cols].astype(F32)).astype(BF16)
    outs.append(pltpu.make_async_copy(dw, dw_out, out_sem.at[2]))
    outs[2].start()
    cols = pl.ds(WIN, REST)
    dr[...] = (d_own[:, cols] + d_recv[0, :, cols].astype(F32) + d_recv[1, :, cols].astype(F32)).astype(BF16)
    outs.append(pltpu.make_async_copy(dr, dr_out, out_sem.at[3]))
    outs[3].start()

    for copy, here in pending:
        if here is None:
            copy.wait_send()
        else:
            pl.when(jnp.logical_not(here))(copy.wait_send)
    for copy in outs:
        copy.wait()


def write_out(*refs):
    ins, outs, held, sem_in, sem_out = refs[:4], refs[4:8], refs[8:12], refs[12], refs[13]
    reads = [pltpu.make_async_copy(ins[i], held[i], sem_in.at[i]) for i in range(4)]
    writes = [pltpu.make_async_copy(held[i], outs[i], sem_out.at[i]) for i in range(4)]
    for copy in reads:
        copy.start()
    for read, write in zip(reads, writes):
        read.wait()
        write.start()
    for copy in writes:
        copy.wait()


def per_device(s, r, fw, fr, aw, ar, tip, bw, br):
    hbm = pl.BlockSpec(memory_space=pl.ANY)
    vmem = pltpu.VMEM
    dma = pltpu.SemaphoreType.DMA
    shapes = (
        jax.ShapeDtypeStruct((BLOCK, WIN), BF16),
        jax.ShapeDtypeStruct((ARROW, WIN), BF16),
        jax.ShapeDtypeStruct((DROWS, WIN), BF16),
        jax.ShapeDtypeStruct((DROWS, REST), BF16),
    )
    outs = pl.pallas_call(
        kernel,
        out_shape=shapes,
        in_specs=[hbm] * 9,
        out_specs=(hbm,) * 4,
        scratch_shapes=[
            vmem((BLOCK, 2048), BF16),
            vmem((4, 16, BLOCK), BF16),
            vmem((4, PIECE, 1024), BF16),
            vmem((1024, FULL), BF16),
            vmem((ARROW, FULL), BF16),
            vmem((ARROW, ARROW), BF16),
            vmem((DROWS, FULL), BF16),
            vmem((3, PIECE, WIN), BF16),
            vmem((PIECE, WIN), F32),
            vmem((PIECE, WIN), BF16),
            vmem((2, PIECE, WIN), BF16),
            vmem((PIECE, WIN), F32),
            vmem((BLOCK, WIN), BF16),
            vmem((WIN, BLOCK), BF16),
            vmem((768, 1024), BF16),
            vmem((2, ARROW, WIN), BF16),
            vmem((WIN, ARROW), BF16),
            vmem((ARROW, WIN), BF16),
            vmem((3, DROWS, FULL), BF16),
            vmem((DROWS, FULL), F32),
            vmem((DROWS, FULL), BF16),
            vmem((2, DROWS, FULL), BF16),
            vmem((DROWS, FULL), F32),
            vmem((DROWS, WIN), BF16),
            vmem((DROWS, REST), BF16),
            dma((7,)),
            dma((S_CHUNKS + 1,)), dma((S_CHUNKS + 1,)),
            dma((12,)), dma((12,)),
            dma((3,)), dma,
            dma((S_CHUNKS, 10)), dma((4,)),
            dma((2, 6)), dma((2, 6)),
            dma((2, 5)), dma((4,)),
            dma((3,)), dma((3,)),
            dma, dma,
            dma((2, 6)), dma((2, 6)),
            dma((4,)),
        ],
        compiler_params=pltpu.CompilerParams(
            collective_id=0, has_side_effects=True, vmem_limit_bytes=60 << 20
        ),
        cost_estimate=pl.CostEstimate(flops=6_800_000_000, bytes_accessed=8_000_000, transcendentals=0),
    )(s[0], r[0].reshape(4, 16, BLOCK), fw[0], fr[0], aw[0], ar[0], tip, bw[0], br[0])
    outs = pl.pallas_call(
        write_out,
        out_shape=shapes,
        in_specs=[hbm] * 4,
        out_specs=(hbm,) * 4,
        scratch_shapes=[vmem(item.shape, BF16) for item in shapes] + [dma((4,)), dma((4,))],
        compiler_params=pltpu.CompilerParams(vmem_limit_bytes=60 << 20),
    )(*outs)
    return tuple(value[None] for value in outs)


def solution(mesh):
    in_specs = (
        P("dom", "row", "col"),
        P("dom", None, "row"),
        P("dom", "row", "col"),
        P("dom", "row", "col"),
        P("dom", None, "col"),
        P("dom", None, "col"),
        P(),
        P("dom", "row", "col"),
        P("dom", "row", "col"),
    )
    out_specs = (
        P("dom", "row", "col"),
        P("dom", None, "col"),
        P("dom", "row", "col"),
        P("dom", "row", "col"),
    )
    return jax.shard_map(
        per_device, mesh=mesh, in_specs=in_specs, out_specs=out_specs, check_vma=False
    )
```

```python
import jax
import jax.numpy as jnp
from jax import lax
from jax.experimental import pallas as pl
from jax.experimental.pallas import tpu as pltpu
from jax.sharding import PartitionSpec as P

MESH = pl.DeviceIdType.MESH
BF16 = jnp.bfloat16
F32 = jnp.float32

BLOCK = 256
WIN = 1536
REST = 512
FULL = WIN + REST
ARROW = 64
DROWS = 192
TOP = 144
PIECE = 272
S_CHUNKS = 4
S_ROWS = BLOCK // S_CHUNKS
TILE = 256


def dot(left, right):
    return jnp.dot(left, right, preferred_element_type=F32)


def al(value, multiple):
    return pl.multiple_of(value, multiple)


def kernel(
    s_in, r_in, fw_in, fr_in, aw_in, ar_in, tip_in, bw_in, br_in,
    x_out, y_out, dw_out, dr_out,
    sz, rz, sg, fg, av, tip, base,
    x_send, x_hold, x_relay, x_recv, x_own, x_neg, xt, xg,
    y_all, yt, y_neg,
    d_send, d_hold, d_relay, d_recv, d_own, dw, dr,
    loc_sem, z_send, z_recv, f_send, f_recv, r_send, r_recv, sa_send, sa_recv,
    xr_send, xr_recv, xa_send, xa_recv, y_send, y_recv, t_send, t_recv,
    dr_send, dr_recv, out_sem,
):
    z = lax.axis_index("dom")
    row = lax.axis_index("row")
    k = lax.axis_index("col")
    y = row // 4
    x = row % 4
    a = (1 - k) * y + k * x
    b = (1 - k) * x + k * y
    stride_a = 4 - 3 * k
    stride_b = 1 + 3 * k

    def at(a_pos, b_pos):
        return {"row": a_pos * stride_a + b_pos * stride_b, "col": k}

    a_next, a_prev = (a + 1) % 4, (a + 3) % 4
    b_next, b_prev, b_opp = (b + 1) % 4, (b + 3) % 4, (b + 2) % 4

    pending = []

    def remote(src, dst, send_sem, recv_sem, device):
        copy = pltpu.make_async_remote_copy(
            src_ref=src, dst_ref=dst, send_sem=send_sem, recv_sem=recv_sem,
            device_id=device, device_id_type=MESH,
        )
        copy.start()
        pending.append((copy, None))
        return copy

    def remote_or_local(src, dst, send_sem, recv_sem, device, here, keep=True):
        copy = pltpu.make_async_remote_copy(
            src_ref=src, dst_ref=dst, send_sem=send_sem, recv_sem=recv_sem,
            device_id=device, device_id_type=MESH,
        )

        @pl.when(here)
        def _():
            pltpu.make_async_copy(src, dst, recv_sem).start()

        @pl.when(jnp.logical_not(here))
        def _():
            copy.start()

        if keep:
            pending.append((copy, here))

    def arrived(ref, sem):
        pltpu.make_async_copy(ref, ref, sem).wait()

    barrier = pltpu.get_barrier_semaphore()
    greeted = 0
    for step in (1, 7):
        pl.semaphore_signal(barrier, inc=1, device_id={"dom": (z + step) % 8}, device_id_type=MESH)
        greeted += 1
    pl.semaphore_signal(barrier, inc=1, device_id={"col": 1 - k}, device_id_type=MESH)
    greeted += 1
    for step in (1, 2, 3):
        for core in (0, 1):
            pl.semaphore_signal(
                barrier, inc=1, device_id={"row": y * 4 + (x + step) % 4, "col": core}, device_id_type=MESH
            )
            pl.semaphore_signal(
                barrier, inc=1, device_id={"row": ((y + step) % 4) * 4 + x, "col": core}, device_id_type=MESH
            )
            greeted += 2

    own_rows = pl.ds(al(a * BLOCK, BLOCK), BLOCK)
    locals_ = [
        pltpu.make_async_copy(fw_in, fg.at[own_rows, pl.ds(0, WIN)], loc_sem.at[0]),
        pltpu.make_async_copy(fr_in, fg.at[own_rows, pl.ds(WIN, REST)], loc_sem.at[1]),
        pltpu.make_async_copy(aw_in, av.at[:, pl.ds(0, WIN)], loc_sem.at[2]),
        pltpu.make_async_copy(ar_in, av.at[:, pl.ds(WIN, REST)], loc_sem.at[3]),
        pltpu.make_async_copy(tip_in, tip, loc_sem.at[4]),
        pltpu.make_async_copy(bw_in, base.at[:, pl.ds(0, WIN)], loc_sem.at[5]),
        pltpu.make_async_copy(br_in, base.at[:, pl.ds(WIN, REST)], loc_sem.at[6]),
    ]
    for copy in locals_:
        copy.start()

    pl.semaphore_wait(barrier, greeted)

    below = {"dom": (z + 7) % 8}
    remote(r_in, rz, z_send.at[S_CHUNKS], z_recv.at[S_CHUNKS], below)
    z_copies = []

    def z_start(chunk):
        rows = pl.ds(chunk * S_ROWS, S_ROWS)
        z_copies.append(remote(s_in.at[rows, :], sz.at[rows, :], z_send.at[chunk], z_recv.at[chunk], below))

    z_start(0)
    z_start(1)

    half = BLOCK // 2

    def block_half(a_pos, part, first, count):
        return fg.at[pl.ds(al(a_pos * BLOCK + part * half, half), half), pl.ds(first, count)]

    def f_own(source, first, count, base_sem):
        for part in (0, 1):
            src = source.at[pl.ds(part * half, half), :]
            remote(src, block_half(a, part, first, count), f_send.at[base_sem + part],
                   f_recv.at[base_sem + part], at(a_next, b))
            src = source.at[pl.ds((1 - part) * half, half), :]
            remote(src, block_half(a, 1 - part, first, count), f_send.at[base_sem + 3 - part],
                   f_recv.at[base_sem + 3 - part], at(a_prev, b))

    def f_forward(first, count, base_sem):
        block = block_half(a_prev, 0, first, count)
        arrived(block, f_recv.at[base_sem])
        remote(block, block, f_send.at[base_sem + 4], f_recv.at[base_sem + 4], at(a_next, b))
        block = block_half(a_next, 1, first, count)
        arrived(block, f_recv.at[base_sem + 3])
        remote(block, block, f_send.at[base_sem + 5], f_recv.at[base_sem + 5], at(a_prev, b))

    def f_rest_of(first, count, base_sem):
        arrived(block_half(a_prev, 1, first, count), f_recv.at[base_sem + 1])
        arrived(block_half(a_next, 0, first, count), f_recv.at[base_sem + 2])
        far = (a + 2) % 4
        arrived(block_half(far, 0, first, count), f_recv.at[base_sem + 4])
        arrived(block_half(far, 1, first, count), f_recv.at[base_sem + 5])

    f_own(fw_in, 0, WIN, 0)

    arrived(rz, z_recv.at[S_CHUNKS])

    @pl.when(z == 7)
    def _():
        rz[...] = jnp.zeros_like(rz)

    r_dst = sg.at[:, pl.ds(128, 16), pl.ds(al(a * BLOCK, BLOCK), BLOCK)]
    for step in (1, 2, 3):
        remote(rz, r_dst, r_send.at[step - 1], r_recv, at((a + step) % 4, b))
    pltpu.make_async_copy(rz, r_dst, r_recv).start()

    def s_spread(chunk):
        first = chunk * S_ROWS
        rows = pl.ds(first, S_ROWS)
        into = pl.ds(first + 16 * (first // 128), S_ROWS)
        arrived(sz.at[rows, :], z_recv.at[chunk])
        if chunk + 2 < S_CHUNKS:
            z_copies[chunk].wait_send()
            pending[:] = [item for item in pending if item[0] is not z_copies[chunk]]
            z_start(chunk + 2)

        @pl.when(z == 7)
        def _():
            sz[rows, :] = jnp.zeros((S_ROWS, 2048), BF16)

        index = 0
        for step in range(4):
            x_to = (x + step) % 4
            for part in range(2):
                src = sz.at[rows, pl.ds(al((part * 4 + x_to) * BLOCK, BLOCK), BLOCK)]
                dst = sg.at[x, into, pl.ds(al((2 * k + part) * BLOCK, BLOCK), BLOCK)]
                device = {"row": y * 4 + x_to, "col": 0}
                sems = (sa_send.at[chunk, index], sa_recv.at[x], device)
                if step:
                    remote(src, dst, *sems)
                else:
                    remote_or_local(src, dst, *sems, k == 0)
                index += 1
        for part in range(2):
            y_to = 2 * k + part
            src = sz.at[rows, pl.ds(part * 1024, 1024)]
            dst = sg.at[y, into, :]
            device = {"row": y_to * 4 + x, "col": 1}
            here = jnp.logical_and(y_to == y, k == 1)
            remote_or_local(src, dst, sa_send.at[chunk, index], sa_recv.at[y], device, here)
            index += 1

    s_spread(0)
    f_forward(0, WIN, 0)
    s_spread(1)
    s_spread(2)
    s_spread(3)

    for copy in locals_:
        copy.wait()
    f_rest_of(0, WIN, 0)
    arrived(sg.at[:, pl.ds(128, 16), :], r_recv)

    def reduce_scatter(width, top, piece, product, send, hold, relay, recv, s_sem, r_sem):
        def part_of(ref, lead, upper, cols):
            rows = pl.ds(0, top) if upper else pl.ds(top, piece - top)
            return ref.at[lead, rows, cols] if lead is not None else ref.at[rows, cols]

        def opposite(c):
            cols = pl.ds(c * width, width)
            send[0, :, cols] = product(b_opp, c).astype(BF16)
            remote(part_of(send, 0, True, cols), part_of(relay, None, True, cols),
                   s_sem.at[c, 0], r_sem.at[c, 0], at(a, b_next))
            remote(part_of(send, 0, False, cols), part_of(relay, None, False, cols),
                   s_sem.at[c, 1], r_sem.at[c, 1], at(a, b_prev))

        def beside(c):
            cols = pl.ds(c * width, width)
            value = product(b_next, c)
            hold[pl.ds(0, top), cols] = value[:top]
            send[1, pl.ds(top, piece - top), cols] = value[top:].astype(BF16)
            remote(part_of(send, 1, False, cols), part_of(recv, 0, False, cols),
                   s_sem.at[c, 2], r_sem.at[c, 2], at(a, b_next))
            value = product(b_prev, c)
            hold[pl.ds(top, piece - top), cols] = value[top:]
            send[2, pl.ds(0, top), cols] = value[:top].astype(BF16)
            remote(part_of(send, 2, True, cols), part_of(recv, 1, True, cols),
                   s_sem.at[c, 3], r_sem.at[c, 3], at(a, b_prev))

        def relayed(c):
            cols = pl.ds(c * width, width)
            arrived(part_of(relay, None, True, cols), r_sem.at[c, 0])
            rows = pl.ds(0, top)
            send[1, rows, cols] = (hold[rows, cols] + relay[rows, cols].astype(F32)).astype(BF16)
            remote(part_of(send, 1, True, cols), part_of(recv, 0, True, cols),
                   s_sem.at[c, 4], r_sem.at[c, 4], at(a, b_next))
            arrived(part_of(relay, None, False, cols), r_sem.at[c, 1])
            rows = pl.ds(top, piece - top)
            send[2, rows, cols] = (hold[rows, cols] + relay[rows, cols].astype(F32)).astype(BF16)
            remote(part_of(send, 2, False, cols), part_of(recv, 1, False, cols),
                   s_sem.at[c, 5], r_sem.at[c, 5], at(a, b_prev))

        def received(c):
            cols = pl.ds(c * width, width)
            arrived(part_of(recv, 0, False, cols), r_sem.at[c, 2])
            arrived(part_of(recv, 1, True, cols), r_sem.at[c, 3])
            arrived(part_of(recv, 0, True, cols), r_sem.at[c, 4])
            arrived(part_of(recv, 1, False, cols), r_sem.at[c, 5])

        return opposite, beside, relayed, received

    x_width = 768
    x_half = 384

    def f_cols(c, part):
        return pl.ds(al(part * x_width + (c + a) % 2 * x_half, 128), x_half)

    def x_product(b_pos, c):
        return jnp.concatenate([dot(sg[b_pos], fg[:, f_cols(c, part)]) for part in range(2)], axis=1)

    opposite, beside, relayed, received = reduce_scatter(
        x_width, TOP, PIECE, x_product, x_send, x_hold, x_relay, x_recv, xr_send, xr_recv
    )

    def x_here(c):
        mine = tip[pl.ds(al(b * 16, 16), 16), :]
        ratio = rz[...].reshape(ARROW, BLOCK)
        for part in range(2):
            cols = pl.ds(c * x_width + part * x_half, x_half)
            right = av[:, f_cols(c, part)]
            value = dot(sg[b], fg[:, f_cols(c, part)])
            arrow = lax.dot_general(ratio, right, (((0,), (0,)), ((), ())), preferred_element_type=F32)
            x_own[pl.ds(0, 128), cols] = value[:128] + arrow[:128]
            x_own[pl.ds(128, 16), cols] = value[128:TOP] + dot(mine, right)
            x_own[pl.ds(TOP, 128), cols] = value[TOP:] + arrow[128:]

    y_rows = pl.ds(al(b * 16, 16), 16)

    def x_final(c):
        received(c)
        if c:
            f_own(fr_in, WIN, REST, 6)
        turn = (c + a) % 2
        for part in range(2):
            cols = pl.ds(c * x_width + part * x_half, x_half)
            into = f_cols(c, part)
            total = x_own[:, cols] + x_recv[0, :, cols].astype(F32) + x_recv[1, :, cols].astype(F32)
            top = total[:128].astype(BF16)
            bottom = total[TOP:].astype(BF16)
            x_neg[pl.ds(0, 128), into] = -top
            x_neg[pl.ds(128, 128), into] = -bottom
            xt[into, pl.ds(0, 128)] = top.T
            xt[into, pl.ds(128, 128)] = bottom.T
            y_all[k, y_rows, into] = total[128:TOP].astype(BF16)
            y_to = 2 * k + part
            remote_or_local(
                xt.at[into, :], xg.at[pl.ds(al(turn * x_half, 128), x_half), pl.ds(al(y * BLOCK, BLOCK), BLOCK)],
                xa_send.at[c, part * 3], xa_recv.at[y], {"row": y_to * 4 + x, "col": 0},
                jnp.logical_and(y_to == y, k == 0),
            )
            for step in range(2):
                x_to = turn * 2 + step
                remote_or_local(
                    xt.at[pl.ds(al(part * x_width + x_to * DROWS, 64), DROWS), :],
                    xg.at[pl.ds(al(y_to * DROWS, 64), DROWS), pl.ds(al(x * BLOCK, BLOCK), BLOCK)],
                    xa_send.at[c, part * 3 + 1 + step], xa_recv.at[x], {"row": y * 4 + x_to, "col": 1},
                    jnp.logical_and(x_to == x, k == 1),
                )

    arrived(sg.at[b_opp, pl.ds(0, BLOCK), :], sa_recv.at[b_opp])
    opposite(0)
    arrived(sg.at[b_next, pl.ds(0, BLOCK), :], sa_recv.at[b_next])
    arrived(sg.at[b_prev, pl.ds(0, BLOCK), :], sa_recv.at[b_prev])
    beside(0)
    opposite(1)
    relayed(0)
    beside(1)
    arrived(sg.at[b, pl.ds(0, BLOCK), :], sa_recv.at[b])
    x_here(0)
    relayed(1)
    x_here(1)
    x_final(0)
    x_final(1)
    outs = [pltpu.make_async_copy(x_neg, x_out, out_sem.at[0])]
    outs[0].start()

    y_mine = y_all.at[k, y_rows, :]
    for step in (1, 2, 3):
        remote(y_mine, y_mine, y_send.at[step - 1], y_recv.at[step - 1], at(a, (b + step) % 4))

    for a_pos in range(4):
        arrived(xg.at[:, pl.ds(a_pos * BLOCK, BLOCK)], xa_recv.at[a_pos])

    d_width = 1024

    def d_product(b_pos, c):
        return dot(xg[pl.ds(al(b_pos * DROWS, 64), DROWS), :], fg[:, pl.ds(c * d_width, d_width)])

    opposite, beside, relayed, received = reduce_scatter(
        d_width, DROWS // 2, DROWS, d_product, d_send, d_hold, d_relay, d_recv, dr_send, dr_recv
    )
    f_forward(WIN, REST, 6)
    opposite(0)
    beside(0)
    f_rest_of(WIN, REST, 6)
    opposite(1)
    for step in (1, 2, 3):
        theirs = y_all.at[k, pl.ds(al(((b + 4 - step) % 4) * 16, 16), 16), :]
        arrived(theirs, y_recv.at[step - 1])
    remote(y_all.at[k], y_all.at[k], t_send, t_recv, {"col": 1 - k})
    relayed(0)
    beside(1)
    y_neg[...] = -y_all[k]
    outs.append(pltpu.make_async_copy(y_neg, y_out, out_sem.at[1]))
    outs[1].start()
    arrived(y_all.at[1 - k], t_recv)
    yt[...] = y_all[row // 8].T

    def d_here(c):
        cols = pl.ds(c * d_width, d_width)
        value = d_product(b, c)
        mine = yt[pl.ds(al((row % 8) * DROWS, 64), DROWS), :]
        d_own[:, cols] = value + base[:, cols].astype(F32) + dot(mine, av[:, cols])

    d_here(0)
    relayed(1)
    d_here(1)

    received(0)
    cols = pl.ds(0, d_width)
    dw[:, cols] = (d_own[:, cols] + d_recv[0, :, cols].astype(F32) + d_recv[1, :, cols].astype(F32)).astype(BF16)
    received(1)
    cols = pl.ds(d_width, WIN - d_width)
    dw[:, cols] = (d_own[:, cols] + d_recv[0, :, cols].astype(F32) + d_recv[1, :, cols].astype(F32)).astype(BF16)
    outs.append(pltpu.make_async_copy(dw, dw_out, out_sem.at[2]))
    outs[2].start()
    cols = pl.ds(WIN, REST)
    dr[...] = (d_own[:, cols] + d_recv[0, :, cols].astype(F32) + d_recv[1, :, cols].astype(F32)).astype(BF16)
    outs.append(pltpu.make_async_copy(dr, dr_out, out_sem.at[3]))
    outs[3].start()

    for copy, here in pending:
        if here is None:
            copy.wait_send()
        else:
            pl.when(jnp.logical_not(here))(copy.wait_send)
    for copy in outs:
        copy.wait()


def write_out(*refs):
    ins, outs, held, sem_in, sem_out = refs[:4], refs[4:8], refs[8:12], refs[12], refs[13]
    reads = [pltpu.make_async_copy(ins[i], held[i], sem_in.at[i]) for i in range(4)]
    writes = [pltpu.make_async_copy(held[i], outs[i], sem_out.at[i]) for i in range(4)]
    for copy in reads:
        copy.start()
    for read, write in zip(reads, writes):
        read.wait()
        write.start()
    for copy in writes:
        copy.wait()


def per_device(s, r, fw, fr, aw, ar, tip, bw, br):
    hbm = pl.BlockSpec(memory_space=pl.ANY)
    vmem = pltpu.VMEM
    dma = pltpu.SemaphoreType.DMA
    shapes = (
        jax.ShapeDtypeStruct((BLOCK, WIN), BF16),
        jax.ShapeDtypeStruct((ARROW, WIN), BF16),
        jax.ShapeDtypeStruct((DROWS, WIN), BF16),
        jax.ShapeDtypeStruct((DROWS, REST), BF16),
    )
    outs = pl.pallas_call(
        kernel,
        out_shape=shapes,
        in_specs=[hbm] * 9,
        out_specs=(hbm,) * 4,
        scratch_shapes=[
            vmem((BLOCK, 2048), BF16),
            vmem((4, 16, BLOCK), BF16),
            vmem((4, PIECE, 1024), BF16),
            vmem((1024, FULL), BF16),
            vmem((ARROW, FULL), BF16),
            vmem((ARROW, ARROW), BF16),
            vmem((DROWS, FULL), BF16),
            vmem((3, PIECE, WIN), BF16),
            vmem((PIECE, WIN), F32),
            vmem((PIECE, WIN), BF16),
            vmem((2, PIECE, WIN), BF16),
            vmem((PIECE, WIN), F32),
            vmem((BLOCK, WIN), BF16),
            vmem((WIN, BLOCK), BF16),
            vmem((768, 1024), BF16),
            vmem((2, ARROW, WIN), BF16),
            vmem((WIN, ARROW), BF16),
            vmem((ARROW, WIN), BF16),
            vmem((3, DROWS, FULL), BF16),
            vmem((DROWS, FULL), F32),
            vmem((DROWS, FULL), BF16),
            vmem((2, DROWS, FULL), BF16),
            vmem((DROWS, FULL), F32),
            vmem((DROWS, WIN), BF16),
            vmem((DROWS, REST), BF16),
            dma((7,)),
            dma((S_CHUNKS + 1,)), dma((S_CHUNKS + 1,)),
            dma((12,)), dma((12,)),
            dma((3,)), dma,
            dma((S_CHUNKS, 10)), dma((4,)),
            dma((2, 6)), dma((2, 6)),
            dma((2, 6)), dma((4,)),
            dma((3,)), dma((3,)),
            dma, dma,
            dma((2, 6)), dma((2, 6)),
            dma((4,)),
        ],
        compiler_params=pltpu.CompilerParams(
            collective_id=0, has_side_effects=True, vmem_limit_bytes=60 << 20
        ),
        cost_estimate=pl.CostEstimate(flops=6_800_000_000, bytes_accessed=8_000_000, transcendentals=0),
    )(s[0], r[0].reshape(4, 16, BLOCK), fw[0], fr[0], aw[0], ar[0], tip, bw[0], br[0])
    outs = pl.pallas_call(
        write_out,
        out_shape=shapes,
        in_specs=[hbm] * 4,
        out_specs=(hbm,) * 4,
        scratch_shapes=[vmem(item.shape, BF16) for item in shapes] + [dma((4,)), dma((4,))],
        compiler_params=pltpu.CompilerParams(vmem_limit_bytes=60 << 20),
    )(*outs)
    return tuple(value[None] for value in outs)


def solution(mesh):
    in_specs = (
        P("dom", "row", "col"),
        P("dom", None, "row"),
        P("dom", "row", "col"),
        P("dom", "row", "col"),
        P("dom", None, "col"),
        P("dom", None, "col"),
        P(),
        P("dom", "row", "col"),
        P("dom", "row", "col"),
    )
    out_specs = (
        P("dom", "row", "col"),
        P("dom", None, "col"),
        P("dom", "row", "col"),
        P("dom", "row", "col"),
    )
    return jax.shard_map(
        per_device, mesh=mesh, in_specs=in_specs, out_specs=out_specs, check_vma=False
    )
```

```python
import jax
import jax.numpy as jnp
from jax import lax
from jax.experimental import pallas as pl
from jax.experimental.pallas import tpu as pltpu
from jax.sharding import PartitionSpec as P

MESH = pl.DeviceIdType.MESH
BF16 = jnp.bfloat16
F32 = jnp.float32

BLOCK = 256
WIN = 1536
REST = 512
FULL = WIN + REST
ARROW = 64
DROWS = 192
TOP = 144
PIECE = 272
S_CHUNKS = 4
S_ROWS = BLOCK // S_CHUNKS
TILE = 256


def dot(left, right):
    return jnp.dot(left, right, preferred_element_type=F32)


def al(value, multiple):
    return pl.multiple_of(value, multiple)


def kernel(
    s_in, r_in, fw_in, fr_in, aw_in, ar_in, tip_in, bw_in, br_in,
    x_out, y_out, dw_out, dr_out,
    sz, rz, sg, fg, av, tip, base,
    x_send, x_hold, x_relay, x_recv, x_own, x_neg, xt, xg,
    y_all, yt, y_neg,
    d_send, d_hold, d_relay, d_recv, d_own, dw, dr,
    loc_sem, z_send, z_recv, f_send, f_recv, r_send, r_recv, sa_send, sa_recv,
    xr_send, xr_recv, xa_send, xa_recv, y_send, y_recv, t_send, t_recv,
    dr_send, dr_recv, out_sem,
):
    z = lax.axis_index("dom")
    row = lax.axis_index("row")
    k = lax.axis_index("col")
    y = row // 4
    x = row % 4
    a = (1 - k) * y + k * x
    b = (1 - k) * x + k * y
    stride_a = 4 - 3 * k
    stride_b = 1 + 3 * k

    def at(a_pos, b_pos):
        return {"row": a_pos * stride_a + b_pos * stride_b, "col": k}

    a_next, a_prev = (a + 1) % 4, (a + 3) % 4
    b_next, b_prev, b_opp = (b + 1) % 4, (b + 3) % 4, (b + 2) % 4

    pending = []

    def remote(src, dst, send_sem, recv_sem, device):
        copy = pltpu.make_async_remote_copy(
            src_ref=src, dst_ref=dst, send_sem=send_sem, recv_sem=recv_sem,
            device_id=device, device_id_type=MESH,
        )
        copy.start()
        pending.append((copy, None))
        return copy

    def remote_or_local(src, dst, send_sem, recv_sem, device, here, keep=True):
        copy = pltpu.make_async_remote_copy(
            src_ref=src, dst_ref=dst, send_sem=send_sem, recv_sem=recv_sem,
            device_id=device, device_id_type=MESH,
        )

        @pl.when(here)
        def _():
            pltpu.make_async_copy(src, dst, recv_sem).start()

        @pl.when(jnp.logical_not(here))
        def _():
            copy.start()

        if keep:
            pending.append((copy, here))

    def arrived(ref, sem):
        pltpu.make_async_copy(ref, ref, sem).wait()

    barrier = pltpu.get_barrier_semaphore()
    greeted = 0
    for step in (1, 7):
        pl.semaphore_signal(barrier, inc=1, device_id={"dom": (z + step) % 8}, device_id_type=MESH)
        greeted += 1
    pl.semaphore_signal(barrier, inc=1, device_id={"col": 1 - k}, device_id_type=MESH)
    greeted += 1
    for step in (1, 2, 3):
        for core in (0, 1):
            pl.semaphore_signal(
                barrier, inc=1, device_id={"row": y * 4 + (x + step) % 4, "col": core}, device_id_type=MESH
            )
            pl.semaphore_signal(
                barrier, inc=1, device_id={"row": ((y + step) % 4) * 4 + x, "col": core}, device_id_type=MESH
            )
            greeted += 2

    own_rows = pl.ds(al(a * BLOCK, BLOCK), BLOCK)
    locals_ = [
        pltpu.make_async_copy(fw_in, fg.at[own_rows, pl.ds(0, WIN)], loc_sem.at[0]),
        pltpu.make_async_copy(fr_in, fg.at[own_rows, pl.ds(WIN, REST)], loc_sem.at[1]),
        pltpu.make_async_copy(aw_in, av.at[:, pl.ds(0, WIN)], loc_sem.at[2]),
        pltpu.make_async_copy(ar_in, av.at[:, pl.ds(WIN, REST)], loc_sem.at[3]),
        pltpu.make_async_copy(tip_in, tip, loc_sem.at[4]),
        pltpu.make_async_copy(bw_in, base.at[:, pl.ds(0, WIN)], loc_sem.at[5]),
        pltpu.make_async_copy(br_in, base.at[:, pl.ds(WIN, REST)], loc_sem.at[6]),
    ]
    for copy in locals_:
        copy.start()

    pl.semaphore_wait(barrier, greeted)

    below = {"dom": (z + 7) % 8}
    remote(r_in, rz, z_send.at[S_CHUNKS], z_recv.at[S_CHUNKS], below)
    z_copies = []

    def z_start(chunk):
        rows = pl.ds(chunk * S_ROWS, S_ROWS)
        z_copies.append(remote(s_in.at[rows, :], sz.at[rows, :], z_send.at[chunk], z_recv.at[chunk], below))

    z_start(0)
    z_start(1)

    half = BLOCK // 2

    def block_half(a_pos, part, first, count):
        return fg.at[pl.ds(al(a_pos * BLOCK + part * half, half), half), pl.ds(first, count)]

    def f_own(source, first, count, base_sem):
        for part in (0, 1):
            src = source.at[pl.ds(part * half, half), :]
            remote(src, block_half(a, part, first, count), f_send.at[base_sem + part],
                   f_recv.at[base_sem + part], at(a_next, b))
            src = source.at[pl.ds((1 - part) * half, half), :]
            remote(src, block_half(a, 1 - part, first, count), f_send.at[base_sem + 3 - part],
                   f_recv.at[base_sem + 3 - part], at(a_prev, b))

    def f_forward(first, count, base_sem):
        block = block_half(a_prev, 0, first, count)
        arrived(block, f_recv.at[base_sem])
        remote(block, block, f_send.at[base_sem + 4], f_recv.at[base_sem + 4], at(a_next, b))
        block = block_half(a_next, 1, first, count)
        arrived(block, f_recv.at[base_sem + 3])
        remote(block, block, f_send.at[base_sem + 5], f_recv.at[base_sem + 5], at(a_prev, b))

    def f_rest_of(first, count, base_sem):
        arrived(block_half(a_prev, 1, first, count), f_recv.at[base_sem + 1])
        arrived(block_half(a_next, 0, first, count), f_recv.at[base_sem + 2])
        far = (a + 2) % 4
        arrived(block_half(far, 0, first, count), f_recv.at[base_sem + 4])
        arrived(block_half(far, 1, first, count), f_recv.at[base_sem + 5])

    f_own(fw_in, 0, WIN, 0)

    arrived(rz, z_recv.at[S_CHUNKS])

    @pl.when(z == 7)
    def _():
        rz[...] = jnp.zeros_like(rz)

    r_dst = sg.at[:, pl.ds(128, 16), pl.ds(al(a * BLOCK, BLOCK), BLOCK)]
    for step in (1, 2, 3):
        remote(rz, r_dst, r_send.at[step - 1], r_recv, at((a + step) % 4, b))
    pltpu.make_async_copy(rz, r_dst, r_recv).start()

    def s_spread(chunk):
        first = chunk * S_ROWS
        rows = pl.ds(first, S_ROWS)
        into = pl.ds(first + 16 * (first // 128), S_ROWS)
        arrived(sz.at[rows, :], z_recv.at[chunk])
        if chunk + 2 < S_CHUNKS:
            z_copies[chunk].wait_send()
            pending[:] = [item for item in pending if item[0] is not z_copies[chunk]]
            z_start(chunk + 2)

        @pl.when(z == 7)
        def _():
            sz[rows, :] = jnp.zeros((S_ROWS, 2048), BF16)

        index = 0
        for step in range(4):
            x_to = (x + step) % 4
            for part in range(2):
                src = sz.at[rows, pl.ds(al((part * 4 + x_to) * BLOCK, BLOCK), BLOCK)]
                dst = sg.at[x, into, pl.ds(al((2 * k + part) * BLOCK, BLOCK), BLOCK)]
                device = {"row": y * 4 + x_to, "col": 0}
                sems = (sa_send.at[chunk, index], sa_recv.at[x], device)
                if step:
                    remote(src, dst, *sems)
                else:
                    remote_or_local(src, dst, *sems, k == 0)
                index += 1
        for part in range(2):
            y_to = 2 * k + part
            src = sz.at[rows, pl.ds(part * 1024, 1024)]
            dst = sg.at[y, into, :]
            device = {"row": y_to * 4 + x, "col": 1}
            here = jnp.logical_and(y_to == y, k == 1)
            remote_or_local(src, dst, sa_send.at[chunk, index], sa_recv.at[y], device, here)
            index += 1

    s_spread(0)
    f_forward(0, WIN, 0)
    s_spread(1)
    s_spread(2)
    s_spread(3)

    for copy in locals_:
        copy.wait()
    f_rest_of(0, WIN, 0)
    arrived(sg.at[:, pl.ds(128, 16), :], r_recv)

    def reduce_scatter(width, top, piece, product, send, hold, relay, recv, s_sem, r_sem):
        def part_of(ref, lead, upper, cols):
            rows = pl.ds(0, top) if upper else pl.ds(top, piece - top)
            return ref.at[lead, rows, cols] if lead is not None else ref.at[rows, cols]

        def opposite(c):
            cols = pl.ds(c * width, width)
            send[0, :, cols] = product(b_opp, c).astype(BF16)
            remote(part_of(send, 0, True, cols), part_of(relay, None, True, cols),
                   s_sem.at[c, 0], r_sem.at[c, 0], at(a, b_next))
            remote(part_of(send, 0, False, cols), part_of(relay, None, False, cols),
                   s_sem.at[c, 1], r_sem.at[c, 1], at(a, b_prev))

        def beside(c):
            cols = pl.ds(c * width, width)
            value = product(b_next, c)
            hold[pl.ds(0, top), cols] = value[:top]
            send[1, pl.ds(top, piece - top), cols] = value[top:].astype(BF16)
            remote(part_of(send, 1, False, cols), part_of(recv, 0, False, cols),
                   s_sem.at[c, 2], r_sem.at[c, 2], at(a, b_next))
            value = product(b_prev, c)
            hold[pl.ds(top, piece - top), cols] = value[top:]
            send[2, pl.ds(0, top), cols] = value[:top].astype(BF16)
            remote(part_of(send, 2, True, cols), part_of(recv, 1, True, cols),
                   s_sem.at[c, 3], r_sem.at[c, 3], at(a, b_prev))

        def relayed(c):
            cols = pl.ds(c * width, width)
            arrived(part_of(relay, None, True, cols), r_sem.at[c, 0])
            rows = pl.ds(0, top)
            send[1, rows, cols] = (hold[rows, cols] + relay[rows, cols].astype(F32)).astype(BF16)
            remote(part_of(send, 1, True, cols), part_of(recv, 0, True, cols),
                   s_sem.at[c, 4], r_sem.at[c, 4], at(a, b_next))
            arrived(part_of(relay, None, False, cols), r_sem.at[c, 1])
            rows = pl.ds(top, piece - top)
            send[2, rows, cols] = (hold[rows, cols] + relay[rows, cols].astype(F32)).astype(BF16)
            remote(part_of(send, 2, False, cols), part_of(recv, 1, False, cols),
                   s_sem.at[c, 5], r_sem.at[c, 5], at(a, b_prev))

        def received(c):
            cols = pl.ds(c * width, width)
            arrived(part_of(recv, 0, False, cols), r_sem.at[c, 2])
            arrived(part_of(recv, 1, True, cols), r_sem.at[c, 3])
            arrived(part_of(recv, 0, True, cols), r_sem.at[c, 4])
            arrived(part_of(recv, 1, False, cols), r_sem.at[c, 5])

        return opposite, beside, relayed, received

    x_width = 768
    x_half = 384

    def f_cols(c, part):
        return pl.ds(al(part * x_width + (c + a) % 2 * x_half, 128), x_half)

    def x_product(b_pos, c):
        return jnp.concatenate([dot(sg[b_pos], fg[:, f_cols(c, part)]) for part in range(2)], axis=1)

    opposite, beside, relayed, received = reduce_scatter(
        x_width, TOP, PIECE, x_product, x_send, x_hold, x_relay, x_recv, xr_send, xr_recv
    )

    def x_here(c):
        mine = tip[pl.ds(al(b * 16, 16), 16), :]
        ratio = rz[...].reshape(ARROW, BLOCK)
        for part in range(2):
            cols = pl.ds(c * x_width + part * x_half, x_half)
            right = av[:, f_cols(c, part)]
            value = dot(sg[b], fg[:, f_cols(c, part)])
            arrow = lax.dot_general(ratio, right, (((0,), (0,)), ((), ())), preferred_element_type=F32)
            x_own[pl.ds(0, 128), cols] = value[:128] + arrow[:128]
            x_own[pl.ds(128, 16), cols] = value[128:TOP] + dot(mine, right)
            x_own[pl.ds(TOP, 128), cols] = value[TOP:] + arrow[128:]

    y_rows = pl.ds(al(b * 16, 16), 16)

    def x_final(c):
        received(c)
        turn = (c + a) % 2
        for part in range(2):
            cols = pl.ds(c * x_width + part * x_half, x_half)
            into = f_cols(c, part)
            total = x_own[:, cols] + x_recv[0, :, cols].astype(F32) + x_recv[1, :, cols].astype(F32)
            top = total[:128].astype(BF16)
            bottom = total[TOP:].astype(BF16)
            x_neg[pl.ds(0, 128), into] = -top
            x_neg[pl.ds(128, 128), into] = -bottom
            xt[into, pl.ds(0, 128)] = top.T
            xt[into, pl.ds(128, 128)] = bottom.T
            y_all[k, y_rows, into] = total[128:TOP].astype(BF16)
            y_to = 2 * k + part
            remote_or_local(
                xt.at[into, :], xg.at[pl.ds(al(turn * x_half, 128), x_half), pl.ds(al(y * BLOCK, BLOCK), BLOCK)],
                xa_send.at[c, part * 3], xa_recv.at[y], {"row": y_to * 4 + x, "col": 0},
                jnp.logical_and(y_to == y, k == 0),
            )
            for step in range(2):
                x_to = turn * 2 + step
                remote_or_local(
                    xt.at[pl.ds(al(part * x_width + x_to * DROWS, 64), DROWS), :],
                    xg.at[pl.ds(al(y_to * DROWS, 64), DROWS), pl.ds(al(x * BLOCK, BLOCK), BLOCK)],
                    xa_send.at[c, part * 3 + 1 + step], xa_recv.at[x], {"row": y * 4 + x_to, "col": 1},
                    jnp.logical_and(x_to == x, k == 1),
                )

    arrived(sg.at[b_opp, pl.ds(0, BLOCK), :], sa_recv.at[b_opp])
    opposite(0)
    arrived(sg.at[b_next, pl.ds(0, BLOCK), :], sa_recv.at[b_next])
    arrived(sg.at[b_prev, pl.ds(0, BLOCK), :], sa_recv.at[b_prev])
    beside(0)
    opposite(1)
    relayed(0)
    beside(1)
    arrived(sg.at[b, pl.ds(0, BLOCK), :], sa_recv.at[b])
    x_here(0)
    relayed(1)
    x_here(1)
    x_final(0)
    x_final(1)
    f_own(fr_in, WIN, REST, 6)
    outs = [pltpu.make_async_copy(x_neg, x_out, out_sem.at[0])]
    outs[0].start()

    y_mine = y_all.at[k, y_rows, :]
    for step in (1, 2, 3):
        remote(y_mine, y_mine, y_send.at[step - 1], y_recv.at[step - 1], at(a, (b + step) % 4))

    for a_pos in range(4):
        arrived(xg.at[:, pl.ds(a_pos * BLOCK, BLOCK)], xa_recv.at[a_pos])

    d_width = 1024

    def d_product(b_pos, c):
        return dot(xg[pl.ds(al(b_pos * DROWS, 64), DROWS), :], fg[:, pl.ds(c * d_width, d_width)])

    opposite, beside, relayed, received = reduce_scatter(
        d_width, DROWS // 2, DROWS, d_product, d_send, d_hold, d_relay, d_recv, dr_send, dr_recv
    )
    opposite(0)
    f_forward(WIN, REST, 6)
    beside(0)
    f_rest_of(WIN, REST, 6)
    opposite(1)
    for step in (1, 2, 3):
        theirs = y_all.at[k, pl.ds(al(((b + 4 - step) % 4) * 16, 16), 16), :]
        arrived(theirs, y_recv.at[step - 1])
    remote(y_all.at[k], y_all.at[k], t_send, t_recv, {"col": 1 - k})
    relayed(0)
    beside(1)
    y_neg[...] = -y_all[k]
    outs.append(pltpu.make_async_copy(y_neg, y_out, out_sem.at[1]))
    outs[1].start()
    arrived(y_all.at[1 - k], t_recv)
    yt[...] = y_all[row // 8].T

    def d_here(c):
        cols = pl.ds(c * d_width, d_width)
        value = d_product(b, c)
        mine = yt[pl.ds(al((row % 8) * DROWS, 64), DROWS), :]
        d_own[:, cols] = value + base[:, cols].astype(F32) + dot(mine, av[:, cols])

    d_here(0)
    relayed(1)
    d_here(1)

    received(0)
    cols = pl.ds(0, d_width)
    dw[:, cols] = (d_own[:, cols] + d_recv[0, :, cols].astype(F32) + d_recv[1, :, cols].astype(F32)).astype(BF16)
    received(1)
    cols = pl.ds(d_width, WIN - d_width)
    dw[:, cols] = (d_own[:, cols] + d_recv[0, :, cols].astype(F32) + d_recv[1, :, cols].astype(F32)).astype(BF16)
    outs.append(pltpu.make_async_copy(dw, dw_out, out_sem.at[2]))
    outs[2].start()
    cols = pl.ds(WIN, REST)
    dr[...] = (d_own[:, cols] + d_recv[0, :, cols].astype(F32) + d_recv[1, :, cols].astype(F32)).astype(BF16)
    outs.append(pltpu.make_async_copy(dr, dr_out, out_sem.at[3]))
    outs[3].start()

    for copy, here in pending:
        if here is None:
            copy.wait_send()
        else:
            pl.when(jnp.logical_not(here))(copy.wait_send)
    for copy in outs:
        copy.wait()


def write_out(*refs):
    ins, outs, held, sem_in, sem_out = refs[:4], refs[4:8], refs[8:12], refs[12], refs[13]
    reads = [pltpu.make_async_copy(ins[i], held[i], sem_in.at[i]) for i in range(4)]
    writes = [pltpu.make_async_copy(held[i], outs[i], sem_out.at[i]) for i in range(4)]
    for copy in reads:
        copy.start()
    for read, write in zip(reads, writes):
        read.wait()
        write.start()
    for copy in writes:
        copy.wait()


def per_device(s, r, fw, fr, aw, ar, tip, bw, br):
    hbm = pl.BlockSpec(memory_space=pl.ANY)
    vmem = pltpu.VMEM
    dma = pltpu.SemaphoreType.DMA
    shapes = (
        jax.ShapeDtypeStruct((BLOCK, WIN), BF16),
        jax.ShapeDtypeStruct((ARROW, WIN), BF16),
        jax.ShapeDtypeStruct((DROWS, WIN), BF16),
        jax.ShapeDtypeStruct((DROWS, REST), BF16),
    )
    outs = pl.pallas_call(
        kernel,
        out_shape=shapes,
        in_specs=[hbm] * 9,
        out_specs=(hbm,) * 4,
        scratch_shapes=[
            vmem((BLOCK, 2048), BF16),
            vmem((4, 16, BLOCK), BF16),
            vmem((4, PIECE, 1024), BF16),
            vmem((1024, FULL), BF16),
            vmem((ARROW, FULL), BF16),
            vmem((ARROW, ARROW), BF16),
            vmem((DROWS, FULL), BF16),
            vmem((3, PIECE, WIN), BF16),
            vmem((PIECE, WIN), F32),
            vmem((PIECE, WIN), BF16),
            vmem((2, PIECE, WIN), BF16),
            vmem((PIECE, WIN), F32),
            vmem((BLOCK, WIN), BF16),
            vmem((WIN, BLOCK), BF16),
            vmem((768, 1024), BF16),
            vmem((2, ARROW, WIN), BF16),
            vmem((WIN, ARROW), BF16),
            vmem((ARROW, WIN), BF16),
            vmem((3, DROWS, FULL), BF16),
            vmem((DROWS, FULL), F32),
            vmem((DROWS, FULL), BF16),
            vmem((2, DROWS, FULL), BF16),
            vmem((DROWS, FULL), F32),
            vmem((DROWS, WIN), BF16),
            vmem((DROWS, REST), BF16),
            dma((7,)),
            dma((S_CHUNKS + 1,)), dma((S_CHUNKS + 1,)),
            dma((12,)), dma((12,)),
            dma((3,)), dma,
            dma((S_CHUNKS, 10)), dma((4,)),
            dma((2, 6)), dma((2, 6)),
            dma((2, 6)), dma((4,)),
            dma((3,)), dma((3,)),
            dma, dma,
            dma((2, 6)), dma((2, 6)),
            dma((4,)),
        ],
        compiler_params=pltpu.CompilerParams(
            collective_id=0, has_side_effects=True, vmem_limit_bytes=60 << 20
        ),
        cost_estimate=pl.CostEstimate(flops=6_800_000_000, bytes_accessed=8_000_000, transcendentals=0),
    )(s[0], r[0].reshape(4, 16, BLOCK), fw[0], fr[0], aw[0], ar[0], tip, bw[0], br[0])
    outs = pl.pallas_call(
        write_out,
        out_shape=shapes,
        in_specs=[hbm] * 4,
        out_specs=(hbm,) * 4,
        scratch_shapes=[vmem(item.shape, BF16) for item in shapes] + [dma((4,)), dma((4,))],
        compiler_params=pltpu.CompilerParams(vmem_limit_bytes=60 << 20),
    )(*outs)
    return tuple(value[None] for value in outs)


def solution(mesh):
    in_specs = (
        P("dom", "row", "col"),
        P("dom", None, "row"),
        P("dom", "row", "col"),
        P("dom", "row", "col"),
        P("dom", None, "col"),
        P("dom", None, "col"),
        P(),
        P("dom", "row", "col"),
        P("dom", "row", "col"),
    )
    out_specs = (
        P("dom", "row", "col"),
        P("dom", None, "col"),
        P("dom", "row", "col"),
        P("dom", "row", "col"),
    )
    return jax.shard_map(
        per_device, mesh=mesh, in_specs=in_specs, out_specs=out_specs, check_vma=False
    )
```
